32 devices in a mesh: dp: 8 (over y, x, core), tensor: 4 (over z).
Axes of the slice: x: 2, y: 2, z: 4, core: 2. Of those that a mesh axis runs over, the one named last changes fastest.
Arguments:
- inputs: bfloat16 [8192, 8192], P('dp', 'tensor'), may hold values from -6 to 6
- frozen_value_weight: bfloat16 [8192, 1024], P('tensor'), may hold values from -0.0625 to 0.0625
- adapter_down_weight: bfloat16 [128, 8192, 64], P('dp', 'tensor'), may hold values from -0.0625 to 0.0625
- adapter_up_weight: bfloat16 [128, 64, 1024], P('dp', None, 'tensor'), may hold values from -0.75 to 0.75
- adapter_per_block: int32 [64], P('dp'), may hold values from 0 to 127, as said below
- adapter_storage_index: int32 [128], replicated, may hold values from 0 to 127, as said below
- value_gradient: bfloat16 [8192, 1024], P('dp', 'tensor'), may hold values from -6 to 6
Outputs:
- values: bfloat16 [8192, 1024], P('dp', 'tensor')
- grad_inputs: bfloat16 [8192, 8192], P('dp', 'tensor')
- grad_down: bfloat16 [128, 8192, 64], P('dp', 'tensor')
- grad_up: bfloat16 [128, 64, 1024], P('dp', None, 'tensor')
The draws below stay inside these ranges and needn't reach their ends.
Inputs may be any that keep to these rules, and one draw needn't show every extreme that they name: Adapter a is kept by data device adapter_storage_index[a] // 16; adapter_storage_index is a permutation. `adapter_per_block`: the 8 blocks of one data device use adapters kept by pairwise different data devices; in every draw there is one data device whose adapters are used by a block of every data device, so that keeper serves all 8 data devices.
All inputs are finite; a program needn't handle non-finite values.
Results may differ from the reference program's by a relative error of at most 0.0054.
Values may be sent and summed in bfloat16 or wider, within the bound.
No kernel may reach another device: no remote copies, remote signals or barrier semaphores. Data moves between devices by JAX's collectives and lax.ppermute only.
A program may use at most 128 MiB of HBM per device.

```python
import jax
import jax.numpy as jnp
from jax import lax

MODEL_WIDTH = 8192
VALUE_WIDTH = 1024
ADAPTER_RANK = 64
BLOCK = 128
ADP_DEV = 16
BLOCKS_DEV = 8
ADAPTER_TOTAL = 128
TOTAL_BLOCKS = 64
ROW_TOTAL = 8192


def layout(key):
    frozen_output = jax.random.fold_in(key, 11)
    k_perm, k_hot, k_noise, k_order, k_slot = jax.random.split(frozen_output, 5)
    owners_count = ADAPTER_TOTAL // ADP_DEV
    index = jax.random.permutation(k_perm, ADAPTER_TOTAL).astype(jnp.int32)
    hot = jax.random.randint(k_hot, (), 0, owners_count)
    owners = jnp.arange(owners_count, dtype=jnp.int32)
    noise = jax.random.randint(k_noise, (owners_count, owners_count), 0, 2 ** 20)
    score = noise * owners_count + owners[None, :] + jnp.where(owners[None, :] == hot, 2 ** 29, 0)
    chosen = jnp.argsort(-score, axis=1)[:, :BLOCKS_DEV].astype(jnp.int32)
    mixing = jax.random.randint(k_order, (owners_count, BLOCKS_DEV), 0, 2 ** 20) * BLOCKS_DEV + jnp.arange(BLOCKS_DEV, dtype=jnp.int32)[None, :]
    reorder = jnp.argsort(mixing, axis=1)
    chosen = jnp.take_along_axis(chosen, reorder, axis=1)
    slots = jax.random.randint(k_slot, (owners_count, BLOCKS_DEV), 0, ADP_DEV)
    spots = (chosen * ADP_DEV + slots).reshape(-1)
    inverse = jnp.argsort(index).astype(jnp.int32)
    return (index, inverse[spots].astype(jnp.int32))


def draw_adapter_storage_index(key, part):
    return layout(key)[0]


def draw_adapter_per_block(key, part):
    return layout(key)[1]


def steps_of(own_key, extent, pieces, low, high):
    factor_of = 1.0
    for dim, shards_of in pieces:
        heights = jax.random.uniform(jax.random.fold_in(jax.random.fold_in(own_key, 6), dim), (shards_of,), jnp.float32, low / len(pieces), high / len(pieces))
        factor_of = factor_of * jnp.repeat(jnp.exp(heights), extent[dim] // shards_of).reshape((-1,) + (1,) * (len(extent) - 1 - dim))
    return factor_of


def bell_draw(key, dims, width, limit, cuts=(), held_as=jnp.bfloat16):
    entries = width * jax.random.normal(key, dims, jnp.float32)
    if cuts:
        entries = entries * steps_of(key, dims, cuts, -0.22, 0.18)
    return jnp.clip(entries, -limit, limit).astype(held_as)


def setup_inputs(seed: int = 0) -> dict:
    arg_keys = jax.random.split(jax.random.key(seed), 8)
    inputs = bell_draw(arg_keys[0], (ROW_TOTAL, MODEL_WIDTH), 1.0, 6.0, ((0, 8), (1, 4)))
    frozen_value_weight = bell_draw(arg_keys[1], (MODEL_WIDTH, VALUE_WIDTH), MODEL_WIDTH ** -0.5, 0.0625, ((0, 4),))
    adapter_down_weight = bell_draw(arg_keys[2], (ADAPTER_TOTAL, MODEL_WIDTH, ADAPTER_RANK), MODEL_WIDTH ** -0.5, 0.0625, ((0, 8), (1, 4)))
    adapter_up_weight = bell_draw(arg_keys[3], (ADAPTER_TOTAL, ADAPTER_RANK, VALUE_WIDTH), ADAPTER_RANK ** -0.5, 0.75, ((0, 8), (2, 4)))
    adapter_per_block = draw_adapter_per_block(jax.random.fold_in(arg_keys[7], 71), 0)
    adapter_storage_index = draw_adapter_storage_index(jax.random.fold_in(arg_keys[7], 71), 0)
    value_gradient = bell_draw(arg_keys[6], (ROW_TOTAL, VALUE_WIDTH), 1.0, 6.0, ((0, 8), (1, 4)))
    return {"inputs": inputs, "frozen_value_weight": frozen_value_weight, "adapter_down_weight": adapter_down_weight, "adapter_up_weight": adapter_up_weight, "adapter_per_block": adapter_per_block, "adapter_storage_index": adapter_storage_index, "value_gradient": value_gradient}


adapter_scale = 0.5


def reference(inputs, frozen_value_weight, adapter_down_weight, adapter_up_weight, adapter_per_block, adapter_storage_index, value_gradient):
    spot = adapter_storage_index[adapter_per_block].astype(jnp.int32)
    x_blocks = inputs.reshape(TOTAL_BLOCKS, BLOCK, MODEL_WIDTH)
    dy_blocks = value_gradient.reshape(TOTAL_BLOCKS, BLOCK, VALUE_WIDTH)

    def step(carry, item):
        acc_down, acc_up = carry
        x_blk, output_gradient_block, row_position = item
        down_matrix = lax.dynamic_index_in_dim(adapter_down_weight, row_position, 0, keepdims=False)
        up_matrix = lax.dynamic_index_in_dim(adapter_up_weight, row_position, 0, keepdims=False)
        low = jnp.dot(x_blk, down_matrix, preferred_element_type=jnp.float32).astype(jnp.bfloat16)
        raised_output = jnp.dot(low, up_matrix, preferred_element_type=jnp.float32)
        low_rank_gradient = (adapter_scale * jnp.dot(output_gradient_block, up_matrix.T, preferred_element_type=jnp.float32)).astype(jnp.bfloat16)
        back = jnp.dot(low_rank_gradient, down_matrix.T, preferred_element_type=jnp.float32)
        term_down = jnp.dot(x_blk.T, low_rank_gradient, preferred_element_type=jnp.float32).astype(jnp.bfloat16)
        term_up = jnp.dot(low.T, output_gradient_block, preferred_element_type=jnp.float32).astype(jnp.bfloat16)
        term_down = lax.optimization_barrier(term_down).astype(jnp.float32)
        term_up = lax.optimization_barrier(term_up).astype(jnp.float32)
        acc_down = acc_down.at[row_position].add(term_down)
        acc_up = acc_up.at[row_position].add(term_up)
        return (acc_down, acc_up), (raised_output, back)

    start = (jnp.zeros((ADAPTER_TOTAL, MODEL_WIDTH, ADAPTER_RANK), jnp.float32), jnp.zeros((ADAPTER_TOTAL, ADAPTER_RANK, VALUE_WIDTH), jnp.float32))
    (acc_down, acc_up), (raised_output, back) = lax.scan(step, start, (x_blocks, dy_blocks, spot))
    frozen_output = jnp.dot(inputs, frozen_value_weight, preferred_element_type=jnp.float32)
    values = (frozen_output + adapter_scale * raised_output.reshape(ROW_TOTAL, VALUE_WIDTH)).astype(jnp.bfloat16)
    grad_base = jnp.dot(value_gradient, frozen_value_weight.T, preferred_element_type=jnp.float32)
    grad_inputs = (grad_base + back.reshape(ROW_TOTAL, MODEL_WIDTH)).astype(jnp.bfloat16)
    return values, grad_inputs, acc_down.astype(jnp.bfloat16), acc_up.astype(jnp.bfloat16)
```

```python
import functools

import jax
import jax.numpy as jnp
from jax import lax
from jax.experimental import pallas as pl
from jax.experimental.pallas import tpu as pltpu
from jax.sharding import PartitionSpec as P

BLOCK = 128
SCALE = 0.5
BF = jnp.bfloat16
F32 = jnp.float32
VMEM_LIMIT = 48 * 1024 * 1024
ALL_VMEM = 62 * 1024 * 1024
LANES = 128

SWAP = [(0, 1), (1, 0), (2, 3), (3, 2)]
FAR_SWAP = [(0, 2), (2, 0), (1, 3), (3, 1)]


def dot(a, b, dims):
    return lax.dot_general(a, b, (dims, ((), ())), preferred_element_type=F32)


def smem():
    return pl.BlockSpec(memory_space=pltpu.SMEM)


def vmem():
    return pl.BlockSpec(memory_space=pltpu.VMEM)


def hbm():
    return pl.BlockSpec(memory_space=pltpu.HBM)


def array(shape, dtype):
    return jax.ShapeDtypeStruct(shape, dtype)


def after(x, *others):
    return lax.optimization_barrier((x,) + others)[0]


def call(kernel, name, out_shape, limit=VMEM_LIMIT, **how):
    return pl.pallas_call(
        kernel,
        out_shape=out_shape,
        compiler_params=pltpu.CompilerParams(vmem_limit_bytes=limit),
        cost_estimate=pl.CostEstimate(flops=0, bytes_accessed=0, transcendentals=0),
        name=name,
        **how,
    )


def copies():
    return pltpu.SemaphoreType.DMA


def request_kernel(nblocks, kept, count_dp, per_block_in, index_in, wanted, keeper, per_block, index, sems):
    started = (
        pltpu.make_async_copy(per_block_in, per_block, sems.at[0]),
        pltpu.make_async_copy(index_in, index, sems.at[1]),
    )
    for copy in started:
        copy.start()
    for copy in started:
        copy.wait()
    row = lax.broadcasted_iota(jnp.int32, (count_dp, 1, LANES), 0)
    value = jnp.full((count_dp, 1, LANES), -1, jnp.int32)
    for b in range(nblocks):
        spot = index[per_block[b]]
        k = lax.div(spot, kept)
        keeper[b] = k
        value = jnp.where(row == k, spot - k * kept, value)
    wanted[...] = value


def request(per_block, index, kept, count_dp):
    nblocks = per_block.shape[0]
    return call(
        functools.partial(request_kernel, nblocks, kept, count_dp),
        "request",
        (array((count_dp, 1, LANES), jnp.int32), array((nblocks,), jnp.int32)),
        in_specs=[hbm(), hbm()],
        out_specs=(vmem(), smem()),
        limit=ALL_VMEM,
        scratch_shapes=[
            pltpu.SMEM(per_block.shape, jnp.int32),
            pltpu.SMEM(index.shape, jnp.int32),
            copies()((2,)),
        ],
    )(per_block, index)


def select_kernel(count_dp, asked, source, out, held, sems):
    moves = []
    for s in range(count_dp):
        copy = pltpu.make_async_copy(
            source.at[jnp.maximum(asked[s, 0, 0], 0)], held.at[s], sems.at[0, s]
        )
        copy.start()
        moves.append((copy, pltpu.make_async_copy(held.at[s], out.at[s], sems.at[1, s])))
    for here, there in moves:
        here.wait()
        there.start()
    for here, there in moves:
        there.wait()


def select(asked, source, count_dp, name):
    shape = (count_dp,) + source.shape[1:]
    return call(
        functools.partial(select_kernel, count_dp),
        name,
        array(shape, BF),
        limit=ALL_VMEM,
        in_specs=[smem(), hbm()],
        out_specs=hbm(),
        scratch_shapes=[pltpu.VMEM(shape, BF), copies()((2, count_dp))],
    )(asked, source)


def low_gradient_kernel(nblocks, keeper, up, dy, part, sent):
    for b in range(nblocks):
        value = SCALE * dot(up[keeper[b]], dy[b * BLOCK:(b + 1) * BLOCK, :], ((1,), (1,)))
        part[b] = value
        sent[b] = value.astype(BF)


def low_gradient(keeper, up, dy):
    nblocks = keeper.shape[0]
    shape = (nblocks, up.shape[1], BLOCK)
    return call(
        functools.partial(low_gradient_kernel, nblocks),
        "low_gradient",
        (array(shape, F32), array(shape, BF)),
        in_specs=[smem(), vmem(), vmem()],
        out_specs=(vmem(), vmem()),
    )(keeper, up, dy)


def low_kernel(nblocks, keeper, down, x, part, sent, downs, xs, sems):
    started = []
    for b in range(nblocks):
        pair = (
            pltpu.make_async_copy(down.at[keeper[b]], downs.at[b], sems.at[0, b]),
            pltpu.make_async_copy(x.at[pl.ds(b * BLOCK, BLOCK)], xs.at[b], sems.at[1, b]),
        )
        for copy in pair:
            copy.start()
        started.append(pair)
    for b in range(nblocks):
        for copy in started[b]:
            copy.wait()
        value = dot(downs[b], xs[b], ((1,), (1,)))
        part[b] = value
        sent[b] = value.astype(BF)


def low_partial(keeper, down, x):
    nblocks = keeper.shape[0]
    _, rank, feat = down.shape
    shape = (nblocks, rank, BLOCK)
    return call(
        functools.partial(low_kernel, nblocks),
        "low_partial",
        (array(shape, F32), array(shape, BF)),
        in_specs=[smem(), hbm(), hbm()],
        out_specs=(vmem(), vmem()),
        scratch_shapes=[
            pltpu.VMEM((nblocks, rank, feat), BF),
            pltpu.VMEM((nblocks, BLOCK, feat), BF),
            copies()((2, nblocks)),
        ],
    )(keeper, down, x)


def total(refs, b):
    value = refs[0][b].astype(F32)
    for ref in refs[1:]:
        value = value + ref[b].astype(F32)
    return value.astype(BF)


def down_terms_kernel(nblocks, addends, keeper, *refs):
    x, terms, grad_low, xs, made, sems = refs[addends:]
    started, sent = [], []
    for b in range(nblocks):
        copy = pltpu.make_async_copy(x.at[pl.ds(b * BLOCK, BLOCK)], xs.at[b], sems.at[0, b])
        copy.start()
        started.append(copy)
    for b in range(nblocks):
        g = total(refs[:addends], b)
        grad_low[b] = g
        started[b].wait()
        made[b] = dot(g, xs[b], ((1,), (0,))).astype(BF)
        copy = pltpu.make_async_copy(made.at[b], terms.at[keeper[b]], sems.at[1, b])
        copy.start()
        sent.append(copy)
    for copy in sent:
        copy.wait()


def down_terms(keeper, grad_low, x, count_dp):
    nblocks = keeper.shape[0]
    rank = grad_low[0].shape[1]
    feat = x.shape[1]
    return call(
        functools.partial(down_terms_kernel, nblocks, len(grad_low)),
        "down_terms",
        (array((count_dp, rank, feat), BF), array((nblocks, rank, BLOCK), BF)),
        limit=ALL_VMEM,
        in_specs=[smem()] + [vmem()] * len(grad_low) + [hbm()],
        out_specs=(hbm(), vmem()),
        scratch_shapes=[
            pltpu.VMEM((nblocks, BLOCK, feat), BF),
            pltpu.VMEM((nblocks, rank, feat), BF),
            copies()((2, nblocks)),
        ],
    )(keeper, *grad_low, x)


def up_terms_kernel(nblocks, addends, keeper, *refs):
    dy, terms, low = refs[addends:]
    for b in range(nblocks):
        value = total(refs[:addends], b)
        low[b] = value
        terms[keeper[b]] = dot(
            value, dy[b * BLOCK:(b + 1) * BLOCK, :], ((1,), (0,))
        ).astype(BF)


def up_terms(keeper, low, dy, count_dp):
    nblocks = keeper.shape[0]
    rank = low[0].shape[1]
    cols = dy.shape[1]
    return call(
        functools.partial(up_terms_kernel, nblocks, len(low)),
        "up_terms",
        (array((count_dp, rank, cols), BF), array((nblocks, rank, BLOCK), BF)),
        in_specs=[smem()] + [vmem()] * (len(low) + 1),
        out_specs=(vmem(), vmem()),
    )(keeper, *low, dy)


def frozen_kernel(runs, z, x, *refs):
    ws, adds, outs = refs[:runs], refs[runs:-runs], refs[-runs:]
    for i in range(runs):
        value = dot(x[...], ws[i][...], ((1,), (0,)))
        if adds:
            value = value + adds[i][...].astype(F32)
        outs[i][...] = value.astype(outs[i].dtype)


def frozen(z, x, w, turns, width, adds, dtype, name):
    rows, feat = x.shape
    tile = 512
    runs = len(turns)
    part = pl.BlockSpec((tile, width), lambda i, z: (i, 0))
    return call(
        functools.partial(frozen_kernel, runs),
        name,
        (array((rows, width), dtype),) * runs,
        limit=ALL_VMEM,
        grid_spec=pltpu.PrefetchScalarGridSpec(
            num_scalar_prefetch=1,
            grid=(rows // tile,),
            in_specs=[pl.BlockSpec((tile, feat), lambda i, z: (i, 0))]
            + [pl.BlockSpec((feat, width), lambda i, z, t=t: (0, z[0] ^ t)) for t in turns]
            + [part] * len(adds),
            out_specs=(part,) * runs,
        ),
    )(z, x, *([w] * runs), *adds)


def values_kernel(nblocks, addends, keeper, *refs):
    low, up, out = refs[addends:]
    for b in range(nblocks):
        rows = slice(b * BLOCK, (b + 1) * BLOCK)
        value = SCALE * dot(low[b], up[keeper[b]], ((0,), (0,)))
        for ref in refs[:addends]:
            value = value + ref[rows, :].astype(F32)
        out[rows, :] = value.astype(BF)


def values_out(keeper, addends, low, up):
    return call(
        functools.partial(values_kernel, low.shape[0], len(addends)),
        "values",
        array(addends[0].shape, BF),
        in_specs=[smem()] + [vmem()] * (len(addends) + 2),
        out_specs=vmem(),
    )(keeper, *addends, low, up)


def grad_inputs_kernel(nblocks, count, z, keeper, *refs):
    pieces = refs[:count]
    w, grad_low, down, out, full = refs[count:]

    @pl.when(pl.program_id(0) == 0)
    def _():
        for turn, piece in enumerate(pieces):
            width = piece.shape[1]
            column = pl.multiple_of((z[0] ^ turn) * width, width)
            full[:, pl.ds(column, width)] = piece[...]

    base = dot(full[...], w[...], ((1,), (1,)))
    for b in range(nblocks):
        rows = slice(b * BLOCK, (b + 1) * BLOCK)
        back = dot(grad_low[b], down[keeper[b]], ((0,), (0,)))
        out[rows, :] = (base[rows, :] + back).astype(BF)


def grad_inputs_out(z, keeper, pieces, w, grad_low, down):
    nblocks, rank, _ = grad_low.shape
    count_dp = down.shape[0]
    rows = pieces[0].shape[0]
    feat, cols = w.shape
    tile = min(512, feat)
    return call(
        functools.partial(grad_inputs_kernel, nblocks, len(pieces)),
        "grad_inputs",
        array((rows, feat), BF),
        grid_spec=pltpu.PrefetchScalarGridSpec(
            num_scalar_prefetch=2,
            grid=(feat // tile,),
            in_specs=[
                pl.BlockSpec(a.shape, lambda i, s, k, n=a.ndim: (0,) * n) for a in pieces
            ]
            + [
                pl.BlockSpec((tile, cols), lambda i, s, k: (i, 0)),
                pl.BlockSpec(grad_low.shape, lambda i, s, k: (0, 0, 0)),
                pl.BlockSpec((count_dp, rank, tile), lambda i, s, k: (0, 0, i)),
            ],
            out_specs=pl.BlockSpec((rows, tile), lambda i, s, k: (0, i)),
            scratch_shapes=[pltpu.VMEM((rows, cols), BF)],
        ),
    )(z, keeper, *pieces, w, grad_low, down)


def collect_kernel(count_dp, kept, asked, terms, out, held, zeros, acc, sems, zero_sems):
    wants = [asked[s, 0, 0] for s in range(count_dp)]
    incoming = [
        pltpu.make_async_copy(terms.at[s], held.at[s], sems.at[0, s]) for s in range(count_dp)
    ]
    for copy in incoming:
        copy.start()
    zeros[...] = jnp.zeros_like(zeros)
    blank = []
    for q in range(kept):
        hits = sum((want == q).astype(jnp.int32) for want in wants)
        blank.append(hits == 0)

        @pl.when(blank[q])
        def _():
            pltpu.make_async_copy(zeros, out.at[q], zero_sems.at[q]).start()

    def send(s):
        return pltpu.make_async_copy(held.at[s], out.at[jnp.maximum(wants[s], 0)], sems.at[1, s])

    leads, shared = [], []
    for s in range(count_dp):
        earlier = jnp.int32(0)
        later = jnp.int32(0)
        for o in range(count_dp):
            same = (wants[o] == wants[s]).astype(jnp.int32)
            if o < s:
                earlier = earlier + same
            if o > s:
                later = later + same
        leads.append((wants[s] >= 0) & (earlier == 0))
        shared.append(later > 0)
        incoming[s].wait()

        @pl.when(leads[s] & ~shared[s])
        def _():
            send(s).start()

    for s in range(count_dp):
        @pl.when(leads[s] & shared[s])
        def _():
            acc[...] = held[s].astype(F32)

            @pl.loop(s + 1, count_dp)
            def _(o):
                @pl.when(asked[o, 0, 0] == wants[s])
                def _():
                    acc[...] += held[o].astype(F32)

            held[s] = acc[...].astype(BF)
            send(s).start()

    for s in range(count_dp):
        @pl.when(leads[s])
        def _():
            send(s).wait()

    for q in range(kept):
        @pl.when(blank[q])
        def _():
            pltpu.make_async_copy(zeros, out.at[q], zero_sems.at[q]).wait()


def collect(asked, terms, kept, name):
    count_dp, rank, width = terms.shape
    return call(
        functools.partial(collect_kernel, count_dp, kept),
        name,
        array((kept, rank, width), BF),
        in_specs=[smem(), hbm()],
        out_specs=hbm(),
        scratch_shapes=[
            pltpu.VMEM((count_dp, rank, width), BF),
            pltpu.VMEM((rank, width), BF),
            pltpu.VMEM((rank, width), F32),
            copies()((2, count_dp)),
            copies()((kept,)),
        ],
    )(asked, terms)


def exchange(a):
    return lax.all_to_all(a, "dp", split_axis=0, concat_axis=0, tiled=True)


def permute(a, pairs):
    return lax.ppermute(a, "tensor", pairs)


def on_line(x, w, down_kept, up_kept, per_block, index, dy):
    count_dp = lax.axis_size("dp")
    z = lax.axis_index("tensor").astype(jnp.int32)[None]
    kept = down_kept.shape[0]
    width = dy.shape[1]

    far_dy = permute(dy, FAR_SWAP)
    near_dy = permute(dy, SWAP)
    wanted, keeper = request(per_block, index, kept, count_dp)
    far_first, near_first = frozen(after(z, wanted), x, w, (3, 1), width, (), BF, "frozen_first")
    asked = exchange(wanted)
    sent_up = select(after(asked, near_first), up_kept, count_dp, "select_up")
    sent_down = select(after(asked, sent_up), down_kept, count_dp, "select_down")
    up = exchange(sent_up)
    part, sent = low_gradient(after(keeper, sent_down), up, dy)
    down = exchange(after(sent_down, part, far_dy, near_dy))

    swapped = permute(sent, SWAP)
    (own,) = frozen(after(z, part), x, w, (0,), width, (), BF, "frozen_own")
    came_far = permute(after(far_first, swapped, own), SWAP)
    part = after(part, own) + swapped
    grad_low_sum = (part, permute(part.astype(BF), FAR_SWAP))
    (far_made,) = frozen(after(z, part), x, w, (2,), width, (came_far,), BF, "frozen_far")
    sent_terms, grad_low = down_terms(after(keeper, far_made), grad_low_sum, x, count_dp)
    got_terms = exchange(sent_terms)
    near_far_dy = permute(after(far_dy, sent_terms), SWAP)

    part, sent = low_partial(after(keeper, grad_low), down, x)
    swapped = permute(sent, SWAP)
    part = part + swapped
    passed = permute(part.astype(BF), FAR_SWAP)
    far_came = permute(after(far_made, passed), FAR_SWAP)
    came_near = permute(after(near_first, passed), SWAP)
    low_sum = (part, passed)
    grad_inputs = grad_inputs_out(
        z, after(keeper, part), (dy, near_dy, far_dy, near_far_dy), w, grad_low, down
    )
    sent_up_terms, low = up_terms(after(keeper, grad_inputs), low_sum, dy, count_dp)
    got_up_terms = exchange(sent_up_terms)
    grad_down = collect(after(asked, sent_up_terms), got_terms, kept, "collect_down")
    values = values_out(after(keeper, grad_down), (own, came_near, far_came), low, up)
    grad_up = collect(after(asked, values), got_up_terms, kept, "collect_up")
    return values, grad_inputs, grad_down, grad_up


def on_ring(x, w, down_kept, up_kept, per_block, index, dy):
    count_dp = lax.axis_size("dp")
    kept = down_kept.shape[0]
    wanted, keeper = request(per_block, index, kept, count_dp)
    asked = exchange(wanted)
    up = exchange(select(asked, up_kept, count_dp, "select_up"))
    down = exchange(select(asked, down_kept, count_dp, "select_down"))
    full_dy = lax.all_gather(dy, "tensor", axis=1, tiled=True)
    none = jnp.zeros((1,), jnp.int32)
    (base,) = frozen(none, x, w, (0,), w.shape[1], (), F32, "frozen_all")
    own = lax.psum_scatter(base, "tensor", scatter_dimension=1, tiled=True)
    grad_low_sum = lax.psum(low_gradient(keeper, up, dy)[0], "tensor")
    sent_terms, grad_low = down_terms(keeper, (grad_low_sum,), x, count_dp)
    got_terms = exchange(sent_terms)
    low_sum = lax.psum(low_partial(keeper, down, x)[0], "tensor")
    sent_up_terms, low = up_terms(keeper, (low_sum,), dy, count_dp)
    got_up_terms = exchange(sent_up_terms)
    grad_inputs = grad_inputs_out(none, keeper, (full_dy,), w, grad_low, down)
    values = values_out(keeper, (own,), low, up)
    grad_down = collect(asked, got_terms, kept, "collect_down")
    grad_up = collect(asked, got_up_terms, kept, "collect_up")
    return values, grad_inputs, grad_down, grad_up


def on_device(
    inputs,
    frozen_value_weight,
    adapter_down_weight,
    adapter_up_weight,
    adapter_per_block,
    adapter_storage_index,
    value_gradient,
):
    run = on_line if lax.axis_size("tensor") == 4 else on_ring
    values, grad_inputs, grad_down, grad_up = run(
        inputs,
        frozen_value_weight,
        jnp.swapaxes(adapter_down_weight, 1, 2),
        adapter_up_weight,
        adapter_per_block,
        adapter_storage_index,
        value_gradient,
    )
    return values, grad_inputs, jnp.swapaxes(grad_down, 1, 2), grad_up


def solution(mesh):
    return jax.shard_map(
        on_device,
        mesh=mesh,
        in_specs=(
            P("dp", "tensor"),
            P("tensor", None),
            P("dp", "tensor", None),
            P("dp", None, "tensor"),
            P("dp"),
            P(),
            P("dp", "tensor"),
        ),
        out_specs=(
            P("dp", "tensor"),
            P("dp", "tensor"),
            P("dp", "tensor", None),
            P("dp", None, "tensor"),
        ),
        check_vma=False,
    )
```

```python
import functools

import jax
import jax.numpy as jnp
from jax import lax
from jax.experimental import pallas as pl
from jax.experimental.pallas import tpu as pltpu
from jax.sharding import PartitionSpec as P

BLOCK = 128
SCALE = 0.5
BF = jnp.bfloat16
F32 = jnp.float32
VMEM_LIMIT = 48 * 1024 * 1024
ALL_VMEM = 57 * 1024 * 1024
LANES = 128

SWAP = [(0, 1), (1, 0), (2, 3), (3, 2)]
FAR_SWAP = [(0, 2), (2, 0), (1, 3), (3, 1)]


def dot(a, b, dims):
    return lax.dot_general(a, b, (dims, ((), ())), preferred_element_type=F32)


def smem():
    return pl.BlockSpec(memory_space=pltpu.SMEM)


def vmem():
    return pl.BlockSpec(memory_space=pltpu.VMEM)


def hbm():
    return pl.BlockSpec(memory_space=pltpu.HBM)


def array(shape, dtype):
    return jax.ShapeDtypeStruct(shape, dtype)


def after(x, *others):
    return lax.optimization_barrier((x,) + others)[0]


def call(kernel, name, out_shape, limit=VMEM_LIMIT, **how):
    return pl.pallas_call(
        kernel,
        out_shape=out_shape,
        compiler_params=pltpu.CompilerParams(vmem_limit_bytes=limit),
        cost_estimate=pl.CostEstimate(flops=0, bytes_accessed=0, transcendentals=0),
        name=name,
        **how,
    )


def copies():
    return pltpu.SemaphoreType.DMA


def request_kernel(nblocks, kept, count_dp, per_block_in, index_in, wanted, keeper, per_block, index, sems):
    started = (
        pltpu.make_async_copy(per_block_in, per_block, sems.at[0]),
        pltpu.make_async_copy(index_in, index, sems.at[1]),
    )
    for copy in started:
        copy.start()
    for copy in started:
        copy.wait()
    row = lax.broadcasted_iota(jnp.int32, (count_dp, 1, LANES), 0)
    value = jnp.full((count_dp, 1, LANES), -1, jnp.int32)
    for b in range(nblocks):
        spot = index[per_block[b]]
        k = lax.div(spot, kept)
        keeper[b] = k
        value = jnp.where(row == k, spot - k * kept, value)
    wanted[...] = value


def request(per_block, index, kept, count_dp):
    nblocks = per_block.shape[0]
    return call(
        functools.partial(request_kernel, nblocks, kept, count_dp),
        "request",
        (array((count_dp, 1, LANES), jnp.int32), array((nblocks,), jnp.int32)),
        in_specs=[hbm(), hbm()],
        out_specs=(vmem(), smem()),
        limit=ALL_VMEM,
        scratch_shapes=[
            pltpu.SMEM(per_block.shape, jnp.int32),
            pltpu.SMEM(index.shape, jnp.int32),
            copies()((2,)),
        ],
    )(per_block, index)


def select_kernel(count_dp, asked, source, out, held, sems):
    moves = []
    for s in range(count_dp):
        copy = pltpu.make_async_copy(
            source.at[jnp.maximum(asked[s, 0, 0], 0)], held.at[s], sems.at[0, s]
        )
        copy.start()
        moves.append((copy, pltpu.make_async_copy(held.at[s], out.at[s], sems.at[1, s])))
    for here, there in moves:
        here.wait()
        there.start()
    for here, there in moves:
        there.wait()


def select(asked, source, count_dp, name):
    shape = (count_dp,) + source.shape[1:]
    return call(
        functools.partial(select_kernel, count_dp),
        name,
        array(shape, BF),
        limit=ALL_VMEM,
        in_specs=[smem(), hbm()],
        out_specs=hbm(),
        scratch_shapes=[pltpu.VMEM(shape, BF), copies()((2, count_dp))],
    )(asked, source)


def low_gradient_kernel(nblocks, keeper, up, dy, part, sent):
    for b in range(nblocks):
        value = SCALE * dot(up[keeper[b]], dy[b * BLOCK:(b + 1) * BLOCK, :], ((1,), (1,)))
        part[b] = value
        sent[b] = value.astype(BF)


def low_gradient(keeper, up, dy):
    nblocks = keeper.shape[0]
    shape = (nblocks, up.shape[1], BLOCK)
    return call(
        functools.partial(low_gradient_kernel, nblocks),
        "low_gradient",
        (array(shape, F32), array(shape, BF)),
        in_specs=[smem(), vmem(), vmem()],
        out_specs=(vmem(), vmem()),
    )(keeper, up, dy)


def low_kernel(nblocks, keeper, down, x, part, sent, downs, xs, sems):
    started = []
    for b in range(nblocks):
        pair = (
            pltpu.make_async_copy(down.at[keeper[b]], downs.at[b], sems.at[0, b]),
            pltpu.make_async_copy(x.at[pl.ds(b * BLOCK, BLOCK)], xs.at[b], sems.at[1, b]),
        )
        for copy in pair:
            copy.start()
        started.append(pair)
    for b in range(nblocks):
        for copy in started[b]:
            copy.wait()
        value = dot(downs[b], xs[b], ((1,), (1,)))
        part[b] = value
        sent[b] = value.astype(BF)


def low_partial(keeper, down, x):
    nblocks = keeper.shape[0]
    _, rank, feat = down.shape
    shape = (nblocks, rank, BLOCK)
    return call(
        functools.partial(low_kernel, nblocks),
        "low_partial",
        (array(shape, F32), array(shape, BF)),
        in_specs=[smem(), hbm(), hbm()],
        out_specs=(vmem(), vmem()),
        scratch_shapes=[
            pltpu.VMEM((nblocks, rank, feat), BF),
            pltpu.VMEM((nblocks, BLOCK, feat), BF),
            copies()((2, nblocks)),
        ],
    )(keeper, down, x)


def total(refs, b):
    value = refs[0][b].astype(F32)
    for ref in refs[1:]:
        value = value + ref[b].astype(F32)
    return value.astype(BF)


def down_terms_kernel(nblocks, addends, keeper, *refs):
    x, terms, grad_low, xs, made, sems = refs[addends:]
    started, sent = [], []
    for b in range(nblocks):
        copy = pltpu.make_async_copy(x.at[pl.ds(b * BLOCK, BLOCK)], xs.at[b], sems.at[0, b])
        copy.start()
        started.append(copy)
    for b in range(nblocks):
        g = total(refs[:addends], b)
        grad_low[b] = g
        started[b].wait()
        made[b] = dot(g, xs[b], ((1,), (0,))).astype(BF)
        copy = pltpu.make_async_copy(made.at[b], terms.at[keeper[b]], sems.at[1, b])
        copy.start()
        sent.append(copy)
    for copy in sent:
        copy.wait()


def down_terms(keeper, grad_low, x, count_dp):
    nblocks = keeper.shape[0]
    rank = grad_low[0].shape[1]
    feat = x.shape[1]
    return call(
        functools.partial(down_terms_kernel, nblocks, len(grad_low)),
        "down_terms",
        (array((count_dp, rank, feat), BF), array((nblocks, rank, BLOCK), BF)),
        limit=ALL_VMEM,
        in_specs=[smem()] + [vmem()] * len(grad_low) + [hbm()],
        out_specs=(hbm(), vmem()),
        scratch_shapes=[
            pltpu.VMEM((nblocks, BLOCK, feat), BF),
            pltpu.VMEM((nblocks, rank, feat), BF),
            copies()((2, nblocks)),
        ],
    )(keeper, *grad_low, x)


def up_terms_kernel(nblocks, addends, keeper, *refs):
    dy, terms, low = refs[addends:]
    for b in range(nblocks):
        value = total(refs[:addends], b)
        low[b] = value
        terms[keeper[b]] = dot(
            value, dy[b * BLOCK:(b + 1) * BLOCK, :], ((1,), (0,))
        ).astype(BF)


def up_terms(keeper, low, dy, count_dp):
    nblocks = keeper.shape[0]
    rank = low[0].shape[1]
    cols = dy.shape[1]
    return call(
        functools.partial(up_terms_kernel, nblocks, len(low)),
        "up_terms",
        (array((count_dp, rank, cols), BF), array((nblocks, rank, BLOCK), BF)),
        in_specs=[smem()] + [vmem()] * (len(low) + 1),
        out_specs=(vmem(), vmem()),
    )(keeper, *low, dy)


def frozen_kernel(runs, z, x, *refs):
    ws, adds, outs = refs[:runs], refs[runs:-runs], refs[-runs:]
    for i in range(runs):
        value = dot(x[...], ws[i][...], ((1,), (0,)))
        if adds:
            value = value + adds[i][...].astype(F32)
        outs[i][...] = value.astype(outs[i].dtype)


def frozen(z, x, w, turns, width, adds, dtype, name):
    rows, feat = x.shape
    tile = 512
    runs = len(turns)
    part = pl.BlockSpec((tile, width), lambda i, z: (i, 0))
    return call(
        functools.partial(frozen_kernel, runs),
        name,
        (array((rows, width), dtype),) * runs,
        limit=ALL_VMEM,
        grid_spec=pltpu.PrefetchScalarGridSpec(
            num_scalar_prefetch=1,
            grid=(rows // tile,),
            in_specs=[pl.BlockSpec((tile, feat), lambda i, z: (i, 0))]
            + [pl.BlockSpec((feat, width), lambda i, z, t=t: (0, z[0] ^ t)) for t in turns]
            + [part] * len(adds),
            out_specs=(part,) * runs,
        ),
    )(z, x, *([w] * runs), *adds)


def grad_inputs_kernel(nblocks, count, z, keeper, *refs):
    pieces = refs[:count]
    w, grad_low, down, out, full = refs[count:]

    @pl.when(pl.program_id(0) == 0)
    def _():
        for turn, piece in enumerate(pieces):
            width = piece.shape[1]
            column = pl.multiple_of((z[0] ^ turn) * width, width)
            full[:, pl.ds(column, width)] = piece[...]

    base = dot(full[...], w[...], ((1,), (1,)))
    for b in range(nblocks):
        rows = slice(b * BLOCK, (b + 1) * BLOCK)
        back = dot(grad_low[b], down[keeper[b]], ((0,), (0,)))
        out[rows, :] = (base[rows, :] + back).astype(BF)


def grad_inputs_out(z, keeper, pieces, w, grad_low, down):
    nblocks, rank, _ = grad_low.shape
    count_dp = down.shape[0]
    rows = pieces[0].shape[0]
    feat, cols = w.shape
    tile = min(512, feat)
    return call(
        functools.partial(grad_inputs_kernel, nblocks, len(pieces)),
        "grad_inputs",
        array((rows, feat), BF),
        grid_spec=pltpu.PrefetchScalarGridSpec(
            num_scalar_prefetch=2,
            grid=(feat // tile,),
            in_specs=[
                pl.BlockSpec(a.shape, lambda i, s, k, n=a.ndim: (0,) * n) for a in pieces
            ]
            + [
                pl.BlockSpec((tile, cols), lambda i, s, k: (i, 0)),
                pl.BlockSpec(grad_low.shape, lambda i, s, k: (0, 0, 0)),
                pl.BlockSpec((count_dp, rank, tile), lambda i, s, k: (0, 0, i)),
            ],
            out_specs=pl.BlockSpec((rows, tile), lambda i, s, k: (0, i)),
            scratch_shapes=[pltpu.VMEM((rows, cols), BF)],
        ),
    )(z, keeper, *pieces, w, grad_low, down)


def collect_body(count_dp, kept, asked, terms, out, held, zeros, acc, sems, zero_sems, beside):
    wants = [asked[s, 0, 0] for s in range(count_dp)]
    incoming = [
        pltpu.make_async_copy(terms.at[s], held.at[s], sems.at[0, s]) for s in range(count_dp)
    ]
    for copy in incoming:
        copy.start()
    zeros[...] = jnp.zeros_like(zeros)
    blank = []
    for q in range(kept):
        hits = sum((want == q).astype(jnp.int32) for want in wants)
        blank.append(hits == 0)

        @pl.when(blank[q])
        def _():
            pltpu.make_async_copy(zeros, out.at[q], zero_sems.at[q]).start()

    beside()

    def send(s):
        return pltpu.make_async_copy(held.at[s], out.at[jnp.maximum(wants[s], 0)], sems.at[1, s])

    leads, shared = [], []
    for s in range(count_dp):
        earlier = jnp.int32(0)
        later = jnp.int32(0)
        for o in range(count_dp):
            same = (wants[o] == wants[s]).astype(jnp.int32)
            if o < s:
                earlier = earlier + same
            if o > s:
                later = later + same
        leads.append((wants[s] >= 0) & (earlier == 0))
        shared.append(later > 0)
        incoming[s].wait()

        @pl.when(leads[s] & ~shared[s])
        def _():
            send(s).start()

    for s in range(count_dp):
        @pl.when(leads[s] & shared[s])
        def _():
            acc[...] = held[s].astype(F32)

            @pl.loop(s + 1, count_dp)
            def _(o):
                @pl.when(asked[o, 0, 0] == wants[s])
                def _():
                    acc[...] += held[o].astype(F32)

            held[s] = acc[...].astype(BF)
            send(s).start()

    for s in range(count_dp):
        @pl.when(leads[s])
        def _():
            send(s).wait()

    for q in range(kept):
        @pl.when(blank[q])
        def _():
            pltpu.make_async_copy(zeros, out.at[q], zero_sems.at[q]).wait()


def collect_kernel(count_dp, kept, asked, terms, out, *scratch):
    collect_body(count_dp, kept, asked, terms, out, *scratch, beside=lambda: None)


def collect_scratch(terms, kept):
    count_dp, rank, width = terms.shape
    return [
        pltpu.VMEM((count_dp, rank, width), BF),
        pltpu.VMEM((rank, width), BF),
        pltpu.VMEM((rank, width), F32),
        copies()((2, count_dp)),
        copies()((kept,)),
    ]


def collect(asked, terms, kept, name):
    count_dp, rank, width = terms.shape
    return call(
        functools.partial(collect_kernel, count_dp, kept),
        name,
        array((kept, rank, width), BF),
        in_specs=[smem(), hbm()],
        out_specs=hbm(),
        scratch_shapes=collect_scratch(terms, kept),
    )(asked, terms)


def values_kernel(nblocks, addends, count_dp, kept, asked, keeper, terms, *refs):
    low, up, out, sums = refs[addends:addends + 4]

    def values():
        for b in range(nblocks):
            rows = slice(b * BLOCK, (b + 1) * BLOCK)
            value = SCALE * dot(low[b], up[keeper[b]], ((0,), (0,)))
            for ref in refs[:addends]:
                value = value + ref[rows, :].astype(F32)
            out[rows, :] = value.astype(BF)

    collect_body(count_dp, kept, asked, terms, sums, *refs[addends + 4:], beside=values)


def values_out(asked, keeper, terms, kept, addends, low, up):
    count_dp, rank, width = terms.shape
    return call(
        functools.partial(values_kernel, low.shape[0], len(addends), count_dp, kept),
        "values",
        (array(addends[0].shape, BF), array((kept, rank, width), BF)),
        in_specs=[smem(), smem(), hbm()] + [vmem()] * (len(addends) + 2),
        out_specs=(vmem(), hbm()),
        scratch_shapes=collect_scratch(terms, kept),
    )(asked, keeper, terms, *addends, low, up)


def exchange(a):
    return lax.all_to_all(a, "dp", split_axis=0, concat_axis=0, tiled=True)


def permute(a, pairs):
    return lax.ppermute(a, "tensor", pairs)


def on_line(x, w, down_kept, up_kept, per_block, index, dy):
    count_dp = lax.axis_size("dp")
    z = lax.axis_index("tensor").astype(jnp.int32)[None]
    kept = down_kept.shape[0]
    width = dy.shape[1]

    far_dy = permute(dy, FAR_SWAP)
    near_dy = permute(dy, SWAP)
    wanted, keeper = request(per_block, index, kept, count_dp)
    asked = exchange(wanted)
    sent_up = select(asked, up_kept, count_dp, "select_up")
    sent_down = select(after(asked, sent_up), down_kept, count_dp, "select_down")
    up = exchange(sent_up)
    part, sent = low_gradient(after(keeper, sent_down), up, dy)
    down = exchange(after(sent_down, part, far_dy, near_dy))

    swapped = permute(sent, SWAP)
    (own,) = frozen(after(z, part), x, w, (0,), width, (), BF, "frozen_own")
    part = after(part, own) + swapped
    passed = permute(part.astype(BF), FAR_SWAP)
    grad_low_sum = (part, passed)
    far_first, near_first = frozen(after(z, part), x, w, (3, 1), width, (), BF, "frozen_first")
    came_far = permute(after(far_first, passed), SWAP)
    sent_terms, grad_low = down_terms(after(keeper, near_first), grad_low_sum, x, count_dp)

    part, sent = low_partial(after(keeper, grad_low), down, x)
    swapped = permute(sent, SWAP)
    got_terms = exchange(after(sent_terms, part, came_far))
    near_far_dy = permute(after(far_dy, part), SWAP)
    part = part + swapped
    passed = permute(part.astype(BF), FAR_SWAP)
    (far_made,) = frozen(after(z, part), x, w, (2,), width, (came_far,), BF, "frozen_far")
    far_came = permute(far_made, FAR_SWAP)
    came_near = permute(after(near_first, passed), SWAP)
    low_sum = (part, passed)
    grad_inputs = grad_inputs_out(
        z, after(keeper, far_made), (dy, near_dy, far_dy, near_far_dy), w, grad_low, down
    )
    sent_up_terms, low = up_terms(after(keeper, grad_inputs), low_sum, dy, count_dp)
    got_up_terms = exchange(sent_up_terms)
    grad_down = collect(after(asked, sent_up_terms), got_terms, kept, "collect_down")
    values, grad_up = values_out(
        after(asked, grad_down), keeper, got_up_terms, kept, (own, came_near, far_came), low, up
    )
    return values, grad_inputs, grad_down, grad_up


def on_ring(x, w, down_kept, up_kept, per_block, index, dy):
    count_dp = lax.axis_size("dp")
    kept = down_kept.shape[0]
    wanted, keeper = request(per_block, index, kept, count_dp)
    asked = exchange(wanted)
    up = exchange(select(asked, up_kept, count_dp, "select_up"))
    down = exchange(select(asked, down_kept, count_dp, "select_down"))
    full_dy = lax.all_gather(dy, "tensor", axis=1, tiled=True)
    none = jnp.zeros((1,), jnp.int32)
    (base,) = frozen(none, x, w, (0,), w.shape[1], (), F32, "frozen_all")
    own = lax.psum_scatter(base, "tensor", scatter_dimension=1, tiled=True)
    grad_low_sum = lax.psum(low_gradient(keeper, up, dy)[0], "tensor")
    sent_terms, grad_low = down_terms(keeper, (grad_low_sum,), x, count_dp)
    got_terms = exchange(sent_terms)
    low_sum = lax.psum(low_partial(keeper, down, x)[0], "tensor")
    sent_up_terms, low = up_terms(keeper, (low_sum,), dy, count_dp)
    got_up_terms = exchange(sent_up_terms)
    grad_inputs = grad_inputs_out(none, keeper, (full_dy,), w, grad_low, down)
    grad_down = collect(asked, got_terms, kept, "collect_down")
    values, grad_up = values_out(asked, keeper, got_up_terms, kept, (own,), low, up)
    return values, grad_inputs, grad_down, grad_up


def on_device(
    inputs,
    frozen_value_weight,
    adapter_down_weight,
    adapter_up_weight,
    adapter_per_block,
    adapter_storage_index,
    value_gradient,
):
    run = on_line if lax.axis_size("tensor") == 4 else on_ring
    values, grad_inputs, grad_down, grad_up = run(
        inputs,
        frozen_value_weight,
        jnp.swapaxes(adapter_down_weight, 1, 2),
        adapter_up_weight,
        adapter_per_block,
        adapter_storage_index,
        value_gradient,
    )
    return values, grad_inputs, jnp.swapaxes(grad_down, 1, 2), grad_up


def solution(mesh):
    return jax.shard_map(
        on_device,
        mesh=mesh,
        in_specs=(
            P("dp", "tensor"),
            P("tensor", None),
            P("dp", "tensor", None),
            P("dp", None, "tensor"),
            P("dp"),
            P(),
            P("dp", "tensor"),
        ),
        out_specs=(
            P("dp", "tensor"),
            P("dp", "tensor"),
            P("dp", "tensor", None),
            P("dp", None, "tensor"),
        ),
        check_vma=False,
    )
```

```python
import functools

import jax
import jax.numpy as jnp
from jax import lax
from jax.experimental import pallas as pl
from jax.experimental.pallas import tpu as pltpu
from jax.sharding import PartitionSpec as P

BLOCK = 128
SCALE = 0.5
BF = jnp.bfloat16
F32 = jnp.float32
VMEM_LIMIT = 48 * 1024 * 1024
ALL_VMEM = 57 * 1024 * 1024
LESS_VMEM = 24 * 1024 * 1024
SMALLER = ("frozen_far",)
LANES = 128

SWAP = [(0, 1), (1, 0), (2, 3), (3, 2)]
FAR_SWAP = [(0, 2), (2, 0), (1, 3), (3, 1)]


def dot(a, b, dims):
    return lax.dot_general(a, b, (dims, ((), ())), preferred_element_type=F32)


def smem():
    return pl.BlockSpec(memory_space=pltpu.SMEM)


def vmem():
    return pl.BlockSpec(memory_space=pltpu.VMEM)


def hbm():
    return pl.BlockSpec(memory_space=pltpu.HBM)


def array(shape, dtype):
    return jax.ShapeDtypeStruct(shape, dtype)


def after(x, *others):
    return lax.optimization_barrier((x,) + others)[0]


def call(kernel, name, out_shape, limit=VMEM_LIMIT, **how):
    return pl.pallas_call(
        kernel,
        out_shape=out_shape,
        compiler_params=pltpu.CompilerParams(vmem_limit_bytes=limit),
        cost_estimate=pl.CostEstimate(flops=0, bytes_accessed=0, transcendentals=0),
        name=name,
        **how,
    )


def copies():
    return pltpu.SemaphoreType.DMA


def request_kernel(nblocks, kept, count_dp, per_block_in, index_in, wanted, keeper, per_block, index, sems):
    started = (
        pltpu.make_async_copy(per_block_in, per_block, sems.at[0]),
        pltpu.make_async_copy(index_in, index, sems.at[1]),
    )
    for copy in started:
        copy.start()
    for copy in started:
        copy.wait()
    row = lax.broadcasted_iota(jnp.int32, (count_dp, 1, LANES), 0)
    value = jnp.full((count_dp, 1, LANES), -1, jnp.int32)
    for b in range(nblocks):
        spot = index[per_block[b]]
        k = lax.div(spot, kept)
        keeper[b] = k
        value = jnp.where(row == k, spot - k * kept, value)
    wanted[...] = value


def request(per_block, index, kept, count_dp):
    nblocks = per_block.shape[0]
    return call(
        functools.partial(request_kernel, nblocks, kept, count_dp),
        "request",
        (array((count_dp, 1, LANES), jnp.int32), array((nblocks,), jnp.int32)),
        in_specs=[hbm(), hbm()],
        out_specs=(vmem(), smem()),
        limit=ALL_VMEM,
        scratch_shapes=[
            pltpu.SMEM(per_block.shape, jnp.int32),
            pltpu.SMEM(index.shape, jnp.int32),
            copies()((2,)),
        ],
    )(per_block, index)


def select_kernel(count_dp, asked, source, out, held, sems):
    moves = []
    for s in range(count_dp):
        copy = pltpu.make_async_copy(
            source.at[jnp.maximum(asked[s, 0, 0], 0)], held.at[s], sems.at[0, s]
        )
        copy.start()
        moves.append((copy, pltpu.make_async_copy(held.at[s], out.at[s], sems.at[1, s])))
    for here, there in moves:
        here.wait()
        there.start()
    for here, there in moves:
        there.wait()


def select(asked, source, count_dp, name):
    shape = (count_dp,) + source.shape[1:]
    return call(
        functools.partial(select_kernel, count_dp),
        name,
        array(shape, BF),
        limit=ALL_VMEM,
        in_specs=[smem(), hbm()],
        out_specs=hbm(),
        scratch_shapes=[pltpu.VMEM(shape, BF), copies()((2, count_dp))],
    )(asked, source)


def low_gradient_kernel(nblocks, keeper, up, dy, part, sent):
    for b in range(nblocks):
        value = SCALE * dot(up[keeper[b]], dy[b * BLOCK:(b + 1) * BLOCK, :], ((1,), (1,)))
        part[b] = value
        sent[b] = value.astype(BF)


def low_gradient(keeper, up, dy):
    nblocks = keeper.shape[0]
    shape = (nblocks, up.shape[1], BLOCK)
    return call(
        functools.partial(low_gradient_kernel, nblocks),
        "low_gradient",
        (array(shape, F32), array(shape, BF)),
        in_specs=[smem(), vmem(), vmem()],
        out_specs=(vmem(), vmem()),
    )(keeper, up, dy)


def low_kernel(nblocks, keeper, down, x, part, sent, downs, xs, sems):
    started = []
    for b in range(nblocks):
        pair = (
            pltpu.make_async_copy(down.at[keeper[b]], downs.at[b], sems.at[0, b]),
            pltpu.make_async_copy(x.at[pl.ds(b * BLOCK, BLOCK)], xs.at[b], sems.at[1, b]),
        )
        for copy in pair:
            copy.start()
        started.append(pair)
    for b in range(nblocks):
        for copy in started[b]:
            copy.wait()
        value = dot(downs[b], xs[b], ((1,), (1,)))
        part[b] = value
        sent[b] = value.astype(BF)


def low_partial(keeper, down, x):
    nblocks = keeper.shape[0]
    _, rank, feat = down.shape
    shape = (nblocks, rank, BLOCK)
    return call(
        functools.partial(low_kernel, nblocks),
        "low_partial",
        (array(shape, F32), array(shape, BF)),
        in_specs=[smem(), hbm(), hbm()],
        out_specs=(vmem(), vmem()),
        scratch_shapes=[
            pltpu.VMEM((nblocks, rank, feat), BF),
            pltpu.VMEM((nblocks, BLOCK, feat), BF),
            copies()((2, nblocks)),
        ],
    )(keeper, down, x)


def total(refs, b):
    value = refs[0][b].astype(F32)
    for ref in refs[1:]:
        value = value + ref[b].astype(F32)
    return value.astype(BF)


def down_terms_kernel(nblocks, addends, keeper, *refs):
    x, terms, grad_low, xs, made, sems = refs[addends:]
    started, sent = [], []
    for b in range(nblocks):
        copy = pltpu.make_async_copy(x.at[pl.ds(b * BLOCK, BLOCK)], xs.at[b], sems.at[0, b])
        copy.start()
        started.append(copy)
    for b in range(nblocks):
        g = total(refs[:addends], b)
        grad_low[b] = g
        started[b].wait()
        made[b] = dot(g, xs[b], ((1,), (0,))).astype(BF)
        copy = pltpu.make_async_copy(made.at[b], terms.at[keeper[b]], sems.at[1, b])
        copy.start()
        sent.append(copy)
    for copy in sent:
        copy.wait()


def down_terms(keeper, grad_low, x, count_dp):
    nblocks = keeper.shape[0]
    rank = grad_low[0].shape[1]
    feat = x.shape[1]
    return call(
        functools.partial(down_terms_kernel, nblocks, len(grad_low)),
        "down_terms",
        (array((count_dp, rank, feat), BF), array((nblocks, rank, BLOCK), BF)),
        limit=ALL_VMEM,
        in_specs=[smem()] + [vmem()] * len(grad_low) + [hbm()],
        out_specs=(hbm(), vmem()),
        scratch_shapes=[
            pltpu.VMEM((nblocks, BLOCK, feat), BF),
            pltpu.VMEM((nblocks, rank, feat), BF),
            copies()((2, nblocks)),
        ],
    )(keeper, *grad_low, x)


def up_terms_kernel(nblocks, addends, keeper, *refs):
    dy, terms, low = refs[addends:]
    for b in range(nblocks):
        value = total(refs[:addends], b)
        low[b] = value
        terms[keeper[b]] = dot(
            value, dy[b * BLOCK:(b + 1) * BLOCK, :], ((1,), (0,))
        ).astype(BF)


def up_terms(keeper, low, dy, count_dp):
    nblocks = keeper.shape[0]
    rank = low[0].shape[1]
    cols = dy.shape[1]
    return call(
        functools.partial(up_terms_kernel, nblocks, len(low)),
        "up_terms",
        (array((count_dp, rank, cols), BF), array((nblocks, rank, BLOCK), BF)),
        in_specs=[smem()] + [vmem()] * (len(low) + 1),
        out_specs=(vmem(), vmem()),
    )(keeper, *low, dy)


def frozen_kernel(runs, z, x, *refs):
    ws, adds, outs = refs[:runs], refs[runs:-runs], refs[-runs:]
    for i in range(runs):
        value = dot(x[...], ws[i][...], ((1,), (0,)))
        if adds:
            value = value + adds[i][...].astype(F32)
        outs[i][...] = value.astype(outs[i].dtype)


def frozen(z, x, w, turns, width, adds, dtype, name):
    rows, feat = x.shape
    tile = 512
    runs = len(turns)
    part = pl.BlockSpec((tile, width), lambda i, z: (i, 0))
    return call(
        functools.partial(frozen_kernel, runs),
        name,
        (array((rows, width), dtype),) * runs,
        limit=LESS_VMEM if name in SMALLER else ALL_VMEM,
        grid_spec=pltpu.PrefetchScalarGridSpec(
            num_scalar_prefetch=1,
            grid=(rows // tile,),
            in_specs=[pl.BlockSpec((tile, feat), lambda i, z: (i, 0))]
            + [pl.BlockSpec((feat, width), lambda i, z, t=t: (0, z[0] ^ t)) for t in turns]
            + [part] * len(adds),
            out_specs=(part,) * runs,
        ),
    )(z, x, *([w] * runs), *adds)


def grad_inputs_kernel(nblocks, count, z, keeper, *refs):
    pieces = refs[:count]
    w, grad_low, down, out, full = refs[count:]

    @pl.when(pl.program_id(0) == 0)
    def _():
        for turn, piece in enumerate(pieces):
            width = piece.shape[1]
            column = pl.multiple_of((z[0] ^ turn) * width, width)
            full[:, pl.ds(column, width)] = piece[...]

    base = dot(full[...], w[...], ((1,), (1,)))
    for b in range(nblocks):
        rows = slice(b * BLOCK, (b + 1) * BLOCK)
        back = dot(grad_low[b], down[keeper[b]], ((0,), (0,)))
        out[rows, :] = (base[rows, :] + back).astype(BF)


def grad_inputs_out(z, keeper, pieces, w, grad_low, down):
    nblocks, rank, _ = grad_low.shape
    count_dp = down.shape[0]
    rows = pieces[0].shape[0]
    feat, cols = w.shape
    tile = min(512, feat)
    return call(
        functools.partial(grad_inputs_kernel, nblocks, len(pieces)),
        "grad_inputs",
        array((rows, feat), BF),
        grid_spec=pltpu.PrefetchScalarGridSpec(
            num_scalar_prefetch=2,
            grid=(feat // tile,),
            in_specs=[
                pl.BlockSpec(a.shape, lambda i, s, k, n=a.ndim: (0,) * n) for a in pieces
            ]
            + [
                pl.BlockSpec((tile, cols), lambda i, s, k: (i, 0)),
                pl.BlockSpec(grad_low.shape, lambda i, s, k: (0, 0, 0)),
                pl.BlockSpec((count_dp, rank, tile), lambda i, s, k: (0, 0, i)),
            ],
            out_specs=pl.BlockSpec((rows, tile), lambda i, s, k: (0, i)),
            scratch_shapes=[pltpu.VMEM((rows, cols), BF)],
        ),
    )(z, keeper, *pieces, w, grad_low, down)


def collect_body(count_dp, kept, asked, terms, out, held, zeros, acc, sems, zero_sems, beside):
    wants = [asked[s, 0, 0] for s in range(count_dp)]
    incoming = [
        pltpu.make_async_copy(terms.at[s], held.at[s], sems.at[0, s]) for s in range(count_dp)
    ]
    for copy in incoming:
        copy.start()
    zeros[...] = jnp.zeros_like(zeros)
    blank = []
    for q in range(kept):
        hits = sum((want == q).astype(jnp.int32) for want in wants)
        blank.append(hits == 0)

        @pl.when(blank[q])
        def _():
            pltpu.make_async_copy(zeros, out.at[q], zero_sems.at[q]).start()

    beside()

    def send(s):
        return pltpu.make_async_copy(held.at[s], out.at[jnp.maximum(wants[s], 0)], sems.at[1, s])

    leads, shared = [], []
    for s in range(count_dp):
        earlier = jnp.int32(0)
        later = jnp.int32(0)
        for o in range(count_dp):
            same = (wants[o] == wants[s]).astype(jnp.int32)
            if o < s:
                earlier = earlier + same
            if o > s:
                later = later + same
        leads.append((wants[s] >= 0) & (earlier == 0))
        shared.append(later > 0)
        incoming[s].wait()

        @pl.when(leads[s] & ~shared[s])
        def _():
            send(s).start()

    for s in range(count_dp):
        @pl.when(leads[s] & shared[s])
        def _():
            acc[...] = held[s].astype(F32)

            @pl.loop(s + 1, count_dp)
            def _(o):
                @pl.when(asked[o, 0, 0] == wants[s])
                def _():
                    acc[...] += held[o].astype(F32)

            held[s] = acc[...].astype(BF)
            send(s).start()

    for s in range(count_dp):
        @pl.when(leads[s])
        def _():
            send(s).wait()

    for q in range(kept):
        @pl.when(blank[q])
        def _():
            pltpu.make_async_copy(zeros, out.at[q], zero_sems.at[q]).wait()


def collect_kernel(count_dp, kept, asked, terms, out, *scratch):
    collect_body(count_dp, kept, asked, terms, out, *scratch, beside=lambda: None)


def collect_scratch(terms, kept):
    count_dp, rank, width = terms.shape
    return [
        pltpu.VMEM((count_dp, rank, width), BF),
        pltpu.VMEM((rank, width), BF),
        pltpu.VMEM((rank, width), F32),
        copies()((2, count_dp)),
        copies()((kept,)),
    ]


def collect(asked, terms, kept, name):
    count_dp, rank, width = terms.shape
    return call(
        functools.partial(collect_kernel, count_dp, kept),
        name,
        array((kept, rank, width), BF),
        in_specs=[smem(), hbm()],
        out_specs=hbm(),
        scratch_shapes=collect_scratch(terms, kept),
    )(asked, terms)


def values_kernel(nblocks, addends, count_dp, kept, asked, keeper, terms, *refs):
    low, up, out, sums = refs[addends:addends + 4]

    def values():
        for b in range(nblocks):
            rows = slice(b * BLOCK, (b + 1) * BLOCK)
            value = SCALE * dot(low[b], up[keeper[b]], ((0,), (0,)))
            for ref in refs[:addends]:
                value = value + ref[rows, :].astype(F32)
            out[rows, :] = value.astype(BF)

    collect_body(count_dp, kept, asked, terms, sums, *refs[addends + 4:], beside=values)


def values_out(asked, keeper, terms, kept, addends, low, up):
    count_dp, rank, width = terms.shape
    return call(
        functools.partial(values_kernel, low.shape[0], len(addends), count_dp, kept),
        "values",
        (array(addends[0].shape, BF), array((kept, rank, width), BF)),
        in_specs=[smem(), smem(), hbm()] + [vmem()] * (len(addends) + 2),
        out_specs=(vmem(), hbm()),
        scratch_shapes=collect_scratch(terms, kept),
    )(asked, keeper, terms, *addends, low, up)


def exchange(a):
    return lax.all_to_all(a, "dp", split_axis=0, concat_axis=0, tiled=True)


def permute(a, pairs):
    return lax.ppermute(a, "tensor", pairs)


def on_line(x, w, down_kept, up_kept, per_block, index, dy):
    count_dp = lax.axis_size("dp")
    z = lax.axis_index("tensor").astype(jnp.int32)[None]
    kept = down_kept.shape[0]
    width = dy.shape[1]

    far_dy = permute(dy, FAR_SWAP)
    near_dy = permute(dy, SWAP)
    wanted, keeper = request(per_block, index, kept, count_dp)
    asked = exchange(wanted)
    sent_up = select(asked, up_kept, count_dp, "select_up")
    sent_down = select(after(asked, sent_up), down_kept, count_dp, "select_down")
    up = exchange(sent_up)
    part, sent = low_gradient(after(keeper, sent_down), up, dy)
    down = exchange(after(sent_down, part, far_dy, near_dy))

    swapped = permute(sent, SWAP)
    (own,) = frozen(after(z, part), x, w, (0,), width, (), BF, "frozen_own")
    part = after(part, own) + swapped
    passed = permute(part.astype(BF), FAR_SWAP)
    grad_low_sum = (part, passed)
    far_first, near_first = frozen(after(z, part), x, w, (3, 1), width, (), BF, "frozen_first")
    came_far = permute(after(far_first, passed), SWAP)
    sent_terms, grad_low = down_terms(after(keeper, near_first), grad_low_sum, x, count_dp)

    part, sent = low_partial(after(keeper, grad_low), down, x)
    swapped = permute(sent, SWAP)
    got_terms = exchange(after(sent_terms, part, came_far))
    near_far_dy = permute(after(far_dy, part), SWAP)
    part = part + swapped
    passed = permute(part.astype(BF), FAR_SWAP)
    (far_made,) = frozen(after(z, part), x, w, (2,), width, (came_far,), BF, "frozen_far")
    far_came = permute(far_made, FAR_SWAP)
    came_near = permute(after(near_first, passed), SWAP)
    low_sum = (part, passed)
    grad_inputs = grad_inputs_out(
        z, after(keeper, far_made), (dy, near_dy, far_dy, near_far_dy), w, grad_low, down
    )
    sent_up_terms, low = up_terms(after(keeper, grad_inputs), low_sum, dy, count_dp)
    got_up_terms = exchange(sent_up_terms)
    grad_down = collect(after(asked, sent_up_terms), got_terms, kept, "collect_down")
    values, grad_up = values_out(
        after(asked, grad_down), keeper, got_up_terms, kept, (own, came_near, far_came), low, up
    )
    return values, grad_inputs, grad_down, grad_up


def on_ring(x, w, down_kept, up_kept, per_block, index, dy):
    count_dp = lax.axis_size("dp")
    kept = down_kept.shape[0]
    wanted, keeper = request(per_block, index, kept, count_dp)
    asked = exchange(wanted)
    up = exchange(select(asked, up_kept, count_dp, "select_up"))
    down = exchange(select(asked, down_kept, count_dp, "select_down"))
    full_dy = lax.all_gather(dy, "tensor", axis=1, tiled=True)
    none = jnp.zeros((1,), jnp.int32)
    (base,) = frozen(none, x, w, (0,), w.shape[1], (), F32, "frozen_all")
    own = lax.psum_scatter(base, "tensor", scatter_dimension=1, tiled=True)
    grad_low_sum = lax.psum(low_gradient(keeper, up, dy)[0], "tensor")
    sent_terms, grad_low = down_terms(keeper, (grad_low_sum,), x, count_dp)
    got_terms = exchange(sent_terms)
    low_sum = lax.psum(low_partial(keeper, down, x)[0], "tensor")
    sent_up_terms, low = up_terms(keeper, (low_sum,), dy, count_dp)
    got_up_terms = exchange(sent_up_terms)
    grad_inputs = grad_inputs_out(none, keeper, (full_dy,), w, grad_low, down)
    grad_down = collect(asked, got_terms, kept, "collect_down")
    values, grad_up = values_out(asked, keeper, got_up_terms, kept, (own,), low, up)
    return values, grad_inputs, grad_down, grad_up


def on_device(
    inputs,
    frozen_value_weight,
    adapter_down_weight,
    adapter_up_weight,
    adapter_per_block,
    adapter_storage_index,
    value_gradient,
):
    run = on_line if lax.axis_size("tensor") == 4 else on_ring
    values, grad_inputs, grad_down, grad_up = run(
        inputs,
        frozen_value_weight,
        jnp.swapaxes(adapter_down_weight, 1, 2),
        adapter_up_weight,
        adapter_per_block,
        adapter_storage_index,
        value_gradient,
    )
    return values, grad_inputs, jnp.swapaxes(grad_down, 1, 2), grad_up


def solution(mesh):
    return jax.shard_map(
        on_device,
        mesh=mesh,
        in_specs=(
            P("dp", "tensor"),
            P("tensor", None),
            P("dp", "tensor", None),
            P("dp", None, "tensor"),
            P("dp"),
            P(),
            P("dp", "tensor"),
        ),
        out_specs=(
            P("dp", "tensor"),
            P("dp", "tensor"),
            P("dp", "tensor", None),
            P("dp", None, "tensor"),
        ),
        check_vma=False,
    )
```
